32 devices in a mesh: seq: 8 (over z, x), head: 4 (over y, core).
Axes of the slice: x: 2, y: 2, z: 4, core: 2. Of those that a mesh axis runs over, the one named last changes fastest.
Arguments:
- inner_input: bfloat16 [4096, 16384], P('seq', 'head'), may hold values from -6 to 6
- state_input: bfloat16 [4096, 4096], P('seq', 'head'), may hold values from -6 to 6
- gate_input: bfloat16 [4096, 16384], P('seq', 'head'), may hold values from -6 to 6
- inner_taps: bfloat16 [4, 16384], P(None, 'head'), may hold values from -3 to 3
- inner_bias: bfloat16 [16384], P('head'), may hold values from -3 to 3
- state_taps: bfloat16 [4, 4096], P(None, 'head'), may hold values from -3 to 3
- state_bias: bfloat16 [4096], P('head'), may hold values from -3 to 3
- step_raw: float32 [256, 4096], P('head', 'seq'), may hold values from -5.3 to -1
- step_bias: float32 [256], P('head'), may hold values from -0.5 to 0.5
- decay_log: float32 [256], P('head'), may hold values from -9 to 1.26
- skip_gain: float32 [256], P('head'), may hold values from 0.5 to 1.5
- norm_gain: bfloat16 [16384], P('head'), may hold values from 0.5 to 1.5
- out_weight: bfloat16 [16384, 4096], P('head', 'seq'), may hold values from -0.0625 to 0.0625
- sequence_lengths: int32 [4], replicated, may hold values from 1 to 2048, 4096 in all
Outputs:
- mixed_out: bfloat16 [4096, 4096], P('seq', 'head')
The draws below stay inside these ranges and needn't reach their ends.
Inputs may be any that keep to these rules, and one draw needn't show every extreme that they name: `sequence_lengths`: the 4 sequences lie end to end in the order given and fill all 4096 positions; the longest has exactly 2048 positions.
All inputs are finite; a program needn't handle non-finite values.
Results may differ from the reference program's by a relative error of at most 0.018.
Values may be sent and summed in bfloat16 or wider, within the bound.
A program may use at most 256 MiB of HBM per device.

```python
import math
from functools import partial
import jax
import jax.numpy as jnp
import numpy as np
from jax import lax

HEAD_COUNT = 256
HEAD_DIM = 64
STATE_DIM = 256
GROUP_COUNT = 8
CONV_WIDTH = 4
BLOCK_LEN = 256
OUT_WIDTH = 4096
SEQ_COUNT = 4
INNER_DIM = 16384
PACKED_TOKENS = 4096
N_HEAD = 4


def draw_step_raw(key, part):
    level_key = jax.random.fold_in(key, 11)
    cluster_random_key = jax.random.fold_in(key, 12)
    noise_levels = jax.random.uniform(level_key, (HEAD_COUNT, PACKED_TOKENS), jnp.float32, -5.3, -3.9)
    sample_locations = jax.random.randint(cluster_random_key, (4,), 0, PACKED_TOKENS)
    token_locations = lax.iota(jnp.int32, PACKED_TOKENS)
    token_clusters = jnp.any(token_locations[None, :] == sample_locations[:, None], axis=0)
    return jnp.where(token_clusters[None, :], -1.0, noise_levels).astype(jnp.float32)


def draw_decay_log(key, part):
    pick_key = jax.random.fold_in(key, 21)
    slow_key = jax.random.fold_in(key, 22)
    fast_key = jax.random.fold_in(key, 23)
    share = 0.5
    slow_pick = jax.random.uniform(pick_key, (HEAD_COUNT,), jnp.float32) < share
    slow_value = jnp.log(20.0 / PACKED_TOKENS) + jnp.log(10.0) * jax.random.uniform(slow_key, (HEAD_COUNT,), jnp.float32)
    fast_value = jnp.log(jax.random.uniform(fast_key, (HEAD_COUNT,), jnp.float32, 2.0, 3.5))
    return jnp.where(slow_pick, slow_value, fast_value).astype(jnp.float32)


def raised(values, rng, source, target, parts, factor):
    def block_of(axis_at):
        return (jnp.arange(values.shape[axis_at]) // (values.shape[axis_at] // parts)).reshape((-1,) + (1,) * (values.ndim - 1 - axis_at))

    near = jax.random.permutation(rng, parts)[block_of(target)]
    second = (block_of(target) + parts // 2) % parts
    return jnp.where((block_of(source) == near) | (block_of(source) == second), factor * values, values)


def level_of(own_key, dims, shards, smallest, high):
    loudness, own = 1.0, jax.random.fold_in(own_key, 6)
    for dim, parts in shards:
        steps = jnp.exp(jax.random.uniform(jax.random.fold_in(own, dim), (parts,), jnp.float32, smallest / len(shards), high / len(shards)))
        loudness = loudness * jnp.repeat(steps, dims[dim] // parts).reshape([-1 if axis == dim else 1 for axis in range(len(dims))])
    return loudness


def length_profile(count, total, most, skew):
    portions = [(1 << 20) // math.isqrt(grade ** skew) + 1 for grade in range(2, count + 1)]
    rest, holding = total - most - (count - 1), [1] * (count - 1)
    while rest > 0:
        movable = [i for i in range(count - 1) if holding[i] < most]
        mass, left = sum([portions[i] for i in movable]), rest
        for i in movable:
            more = min(most - holding[i], max(1, left * portions[i] // mass), rest)
            holding[i] = holding[i] + more
            rest = rest - more
    return np.array([most] + holding)


def uneven(rng, number_of, total, most, skew):
    if number_of == 2:
        one = jax.random.randint(rng, (), max(1, total - most), min(most, total - 1) + 1)
        return jnp.stack([one, total - one])
    lengths = jnp.asarray(length_profile(number_of, total, most, skew), jnp.int32)
    twos = (number_of - 1) // 2
    donor, taker = lengths[1:1 + 2 * twos:2], lengths[2:2 + 2 * twos:2]
    room = jnp.minimum(donor - 1, most - taker)
    passed = jax.random.randint(jax.random.fold_in(rng, 1), (twos,), 0, 1 << 20) % (room + 1)
    lengths = lengths.at[1:1 + 2 * twos:2].set(donor - passed).at[2:2 + 2 * twos:2].set(taker + passed)
    return lengths[jax.random.permutation(jax.random.fold_in(rng, 2), number_of)]


def bell_draw(stream_key, dims, scale, bound, shards=(), held_as=jnp.bfloat16):
    drawn = scale * jax.random.normal(stream_key, dims, jnp.float32)
    if shards:
        drawn = drawn * level_of(stream_key, dims, shards, -0.22, 0.18)
    return jnp.clip(drawn, -bound, bound).astype(held_as)


def noise_with(own_key, extent, deviation, limit, pieces, heavy, held_as=jnp.bfloat16):
    array = deviation * jax.random.normal(own_key, extent, jnp.float32)
    if pieces:
        array = array * level_of(own_key, extent, pieces, -0.22, 0.18)
    return jnp.clip(raised(array, jax.random.fold_in(own_key, 3), *heavy), -limit, limit).astype(held_as)


def setup_inputs(seed: int = 0) -> dict:
    splits = jax.random.split(jax.random.key(seed), 15)
    return {
        "inner_input": bell_draw(splits[0], (PACKED_TOKENS, INNER_DIM), 1.0, 6.0, ((0, 8), (1, 4))),
        "state_input": bell_draw(splits[1], (PACKED_TOKENS, GROUP_COUNT * 2 * STATE_DIM), 1.0, 6.0, ((0, 8), (1, 4))),
        "gate_input": bell_draw(splits[2], (PACKED_TOKENS, INNER_DIM), 1.0, 6.0, ((0, 8), (1, 4))),
        "inner_taps": bell_draw(splits[3], (CONV_WIDTH, INNER_DIM), CONV_WIDTH ** -0.5, 3.0, ((1, 4),)),
        "inner_bias": bell_draw(splits[4], (INNER_DIM,), 0.5, 3.0, ((0, 4),)),
        "state_taps": bell_draw(splits[5], (CONV_WIDTH, GROUP_COUNT * 2 * STATE_DIM), CONV_WIDTH ** -0.5, 3.0, ((1, 4),)),
        "state_bias": bell_draw(splits[6], (GROUP_COUNT * 2 * STATE_DIM,), 0.5, 3.0, ((0, 4),)),
        "step_raw": draw_step_raw(jax.random.fold_in(splits[14], 71), 0),
        "step_bias": jnp.clip(jax.random.uniform(splits[8], (HEAD_COUNT,), jnp.float32, -0.5, 0.5) * level_of(splits[8], (HEAD_COUNT,), ((0, 4),), -0.4, 0.0), -0.5, 0.5),
        "decay_log": draw_decay_log(jax.random.fold_in(splits[14], 71), 0),
        "skip_gain": jnp.clip(0.5 + 1.0 * jax.random.uniform(splits[10], (HEAD_COUNT,), jnp.float32) ** level_of(splits[10], (HEAD_COUNT,), ((0, 4),), -0.2, 0.2), 0.5, 1.5),
        "norm_gain": jnp.clip(1.0 + 0.1 * jax.random.normal(splits[11], (INNER_DIM,), jnp.float32), 0.5, 1.5).astype(jnp.bfloat16),
        "out_weight": noise_with(splits[12], (INNER_DIM, OUT_WIDTH), INNER_DIM ** -0.5, 0.0625, ((0, 4), (1, 8)), (0, 1, 8, 2.0)),
        "sequence_lengths": uneven(splits[13], SEQ_COUNT, PACKED_TOKENS, PACKED_TOKENS // 2, 2).astype(jnp.int32),
    }


HIGHEST = lax.Precision.HIGHEST
EPSILON = 1e-05

def segment_of(positions, sequence_lengths):
    starts = jnp.cumsum(sequence_lengths) - sequence_lengths
    hits = (positions[:, None] >= starts[None, :]).astype(jnp.int32)
    return lax.optimization_barrier(jnp.sum(hits, axis=1)) - 1

def causal_conv(extended, seg_extended, tap_table, bias_row):
    tap_count = tap_table.shape[0]
    length = extended.shape[0] - tap_count + 1
    current = seg_extended[tap_count - 1:]
    summed = jnp.zeros((length, bias_row.shape[0]), jnp.float32) + bias_row.astype(jnp.float32)
    for start_shift in range(tap_count):
        kept_mask = (seg_extended[start_shift:start_shift + length] == current).astype(jnp.float32)
        summed = summed + tap_table[start_shift].astype(jnp.float32) * extended[start_shift:start_shift + length].astype(jnp.float32) * kept_mask[:, None]
    return jax.nn.silu(summed).astype(jnp.bfloat16)

def block_step(decay_rates, skip_gains, carried, inputs):
    state_now, seg_before = carried
    input_block, write_block, read_block, step_block, seg_block = inputs
    block_rows = input_block.shape[0]
    log_decay = -decay_rates[..., None] * step_block
    running = jnp.cumsum(log_decay, axis=2)
    input_vals = input_block.astype(jnp.float32)
    write_vecs = write_block.astype(jnp.float32)
    read_vecs = read_block.astype(jnp.float32)
    scores = jnp.einsum('ign,jgn->gij', read_vecs, write_vecs, precision=HIGHEST)
    row_index = lax.broadcasted_iota(jnp.int32, (block_rows, block_rows), 0)
    col_index = lax.broadcasted_iota(jnp.int32, (block_rows, block_rows), 1)
    linked = (row_index >= col_index) & (seg_block[:, None] == seg_block[None, :])
    spread = running[..., :, None] - running[..., None, :]
    decays = jnp.where(linked, jnp.exp(jnp.where(linked, spread, 0.0)), 0.0)
    scaled = input_vals * jnp.transpose(step_block, (2, 0, 1))[..., None]
    within = jnp.einsum('ghij,jghp->ighp', decays * scores[:, None], scaled, precision=HIGHEST)
    alive_mask = (seg_block == seg_before).astype(jnp.float32)
    entering = jnp.transpose(alive_mask * jnp.exp(running), (2, 0, 1))
    carried_out = jnp.einsum('ign,ghpn->ighp', read_vecs, state_now, precision=HIGHEST) * entering[..., None]
    outputs = within + carried_out + skip_gains[..., None] * input_vals
    last_seg = seg_block[block_rows - 1]
    closing = (seg_block == last_seg).astype(jnp.float32) * jnp.exp(running[..., block_rows - 1:] - running)
    weighted = scaled * jnp.transpose(closing, (2, 0, 1))[..., None]
    kept = (alive_mask[block_rows - 1] * jnp.exp(running[..., block_rows - 1]))[..., None, None]
    new_state = kept * state_now + jnp.einsum('jghp,jgn->ghpn', weighted, write_vecs, precision=HIGHEST)
    return ((new_state, last_seg), outputs)

def reference(inner_input, state_input, gate_input, inner_taps, inner_bias, state_taps, state_bias, step_raw, step_bias, decay_log, skip_gain, norm_gain, out_weight, sequence_lengths):
    positions = lax.iota(jnp.int32, PACKED_TOKENS + CONV_WIDTH - 1) - (CONV_WIDTH - 1)
    seg_extended = segment_of(positions, sequence_lengths)
    seg_local = seg_extended[CONV_WIDTH - 1:]
    group_width = INNER_DIM // GROUP_COUNT
    group_heads = HEAD_COUNT // GROUP_COUNT
    pair_width = 2 * STATE_DIM
    block_count = PACKED_TOKENS // BLOCK_LEN

    def one_group(items):
        inner_part, state_part, gate_part, inner_tap, inner_off, state_tap, state_off, raw_part, bias_part, log_part, residual_skip_term, gain_part = items
        pad_inner = jnp.zeros((CONV_WIDTH - 1, group_width), jnp.bfloat16)
        inner_conv = causal_conv(jnp.concatenate([pad_inner, inner_part]), seg_extended, inner_tap, inner_off)
        pad_state = jnp.zeros((CONV_WIDTH - 1, pair_width), jnp.bfloat16)
        state_conv = causal_conv(jnp.concatenate([pad_state, state_part]), seg_extended, state_tap, state_off)
        vectors = state_conv.reshape(PACKED_TOKENS, 1, 2, STATE_DIM)
        steps_all = jax.nn.softplus(raw_part + bias_part[:, None]).reshape(1, group_heads, PACKED_TOKENS)
        decay_rates = jnp.exp(log_part).reshape(1, group_heads)
        sequence = (inner_conv.reshape(block_count, BLOCK_LEN, 1, group_heads, HEAD_DIM), vectors[:, :, 0].reshape(block_count, BLOCK_LEN, 1, STATE_DIM), vectors[:, :, 1].reshape(block_count, BLOCK_LEN, 1, STATE_DIM), jnp.transpose(steps_all.reshape(1, group_heads, block_count, BLOCK_LEN), (2, 0, 1, 3)), seg_local.reshape(block_count, BLOCK_LEN))
        start_carry = (jnp.zeros((1, group_heads, HEAD_DIM, STATE_DIM), jnp.float32), seg_extended[CONV_WIDTH - 2])
        stepper = partial(block_step, decay_rates, residual_skip_term.reshape(1, group_heads))
        _, outputs = lax.scan(stepper, start_carry, sequence)
        y_all = outputs.reshape(PACKED_TOKENS, group_width)
        gated = y_all * jax.nn.silu(gate_part.astype(jnp.float32))
        mean_sq = lax.optimization_barrier(jnp.mean(gated * gated, axis=1, keepdims=True))
        return (gated * lax.rsqrt(mean_sq + EPSILON) * gain_part.astype(jnp.float32)).astype(jnp.bfloat16)
    items = (jnp.transpose(inner_input.reshape(PACKED_TOKENS, GROUP_COUNT, group_width), (1, 0, 2)), jnp.transpose(state_input.reshape(PACKED_TOKENS, GROUP_COUNT, pair_width), (1, 0, 2)), jnp.transpose(gate_input.reshape(PACKED_TOKENS, GROUP_COUNT, group_width), (1, 0, 2)), jnp.transpose(inner_taps.reshape(CONV_WIDTH, GROUP_COUNT, group_width), (1, 0, 2)), inner_bias.reshape(GROUP_COUNT, group_width), jnp.transpose(state_taps.reshape(CONV_WIDTH, GROUP_COUNT, pair_width), (1, 0, 2)), state_bias.reshape(GROUP_COUNT, pair_width), step_raw.reshape(GROUP_COUNT, group_heads, PACKED_TOKENS), step_bias.reshape(GROUP_COUNT, group_heads), decay_log.reshape(GROUP_COUNT, group_heads), skip_gain.reshape(GROUP_COUNT, group_heads), norm_gain.reshape(GROUP_COUNT, group_width))
    normed_groups = lax.map(one_group, items)
    per_block = GROUP_COUNT // N_HEAD
    normed_sets = normed_groups.reshape(N_HEAD, per_block, PACKED_TOKENS, group_width)
    weight_sets = out_weight.reshape(N_HEAD, per_block, group_width, OUT_WIDTH)

    def add_block(total_sum, pair):
        normed_set, weight_set = pair
        partial_sum = jnp.zeros((PACKED_TOKENS, OUT_WIDTH), jnp.float32)
        for member in range(per_block):
            partial_sum = partial_sum + jnp.dot(normed_set[member], weight_set[member], preferred_element_type=jnp.float32)
        rounded = lax.optimization_barrier(partial_sum.astype(jnp.bfloat16))
        return (total_sum + rounded.astype(jnp.float32), None)
    total_sum, _ = lax.scan(add_block, jnp.zeros((PACKED_TOKENS, OUT_WIDTH), jnp.float32), (normed_sets, weight_sets))
    return total_sum.astype(jnp.bfloat16)
```

```python
from functools import partial

import jax
import jax.numpy as jnp
from jax import lax
from jax.experimental import pallas as pl
from jax.experimental.pallas import tpu as pltpu
from jax.sharding import PartitionSpec as P

HEAD_DIM = 64
STATE_DIM = 256
HALO = 16
TILE = 256
STEP_HEADS = 8
LOG2E = 1.4426950408889634
SEGMENT_DROP = 200.0
EPSILON = 1e-05
BF16 = jnp.bfloat16
F32 = jnp.float32


def segment_of(positions, sequence_lengths):
    starts = jnp.cumsum(sequence_lengths) - sequence_lengths
    hits = (positions[:, None] >= starts[None, :]).astype(jnp.int32)
    return jnp.sum(hits, axis=1) - 1


def silu(v):
    return v * (0.5 * jnp.tanh(0.5 * v) + 0.5)


def conv(values, halo, masks, taps, bias):
    now = values.astype(F32)
    extended = jnp.concatenate([halo.astype(F32), now], axis=0)
    total = bias + taps[3:4] * now
    for back in range(1, 4):
        shifted = pltpu.roll(extended, back, 0)[HALO:]
        total = total + taps[3 - back : 4 - back] * (shifted * masks[:, back - 1 : back])
    return silu(total).astype(BF16)


def spread_matrix(rows, width, first_head, heads):
    row = lax.broadcasted_iota(jnp.int32, (rows, width), 0)
    col = lax.broadcasted_iota(jnp.int32, (rows, width), 1)
    return (row % heads == first_head + col // HEAD_DIM).astype(F32).astype(BF16)


def local_kernel(
    per_group_steps,
    x_ref,
    xh_ref,
    xt_ref,
    xb_ref,
    s_ref,
    sh_ref,
    st_ref,
    sb_ref,
    mask_ref,
    col_ref,
    row_ref,
    close_ref,
    skip_ref,
    y_ref,
    end_ref,
    read_ref,
    score_ref,
    write_ref,
):
    tokens = x_ref.shape[0]

    @pl.when(pl.program_id(0) % per_group_steps == 0)
    def _():
        masks = mask_ref[...]
        for part in range(2 * STATE_DIM // 128):
            lanes = slice(part * 128, part * 128 + 128)
            vec = conv(
                s_ref[:, lanes], sh_ref[:, lanes], masks, st_ref[:, lanes], sb_ref[:, lanes]
            )
            if part * 128 < STATE_DIM:
                write_ref[:, lanes] = vec
            else:
                read_ref[:, part * 128 - STATE_DIM : part * 128 - STATE_DIM + 128] = vec
        for at in range(0, tokens, TILE):
            score = lax.dot_general(
                read_ref[at : at + TILE, :],
                write_ref[: at + TILE, :],
                (((1,), (1,)), ((), ())),
                preferred_element_type=F32,
            )
            row = lax.broadcasted_iota(jnp.int32, score.shape, 0) + at
            col = lax.broadcasted_iota(jnp.int32, score.shape, 1)
            score_ref[at : at + TILE, : at + TILE] = jnp.where(row >= col, score, 0.0)

    masks = mask_ref[...]
    close = close_ref[0]
    for pair in range(STEP_HEADS // 2):
        lanes = slice(pair * 128, pair * 128 + 128)
        u = conv(x_ref[:, lanes], xh_ref[:, lanes], masks, xt_ref[:, lanes], xb_ref[:, lanes])
        weight = jnp.dot(
            close,
            spread_matrix(2 * STEP_HEADS, 128, 2 * pair, STEP_HEADS),
            preferred_element_type=F32,
        )
        weighted = (u.astype(F32) * weight).astype(BF16)
        end_ref[lanes, :] = lax.dot_general(
            weighted, write_ref[...], (((0,), (0,)), ((), ())), preferred_element_type=F32
        ).astype(BF16)
        for at in range(0, tokens, TILE):
            rows = slice(at, at + TILE)
            pieces = []
            for head in (2 * pair, 2 * pair + 1):
                here = col_ref[0, rows, head : head + 1]
                total = jnp.zeros((TILE, 128), F32)
                for back in range(0, at + TILE, TILE):
                    cols = slice(back, back + TILE)
                    gap = jnp.minimum(here - row_ref[head : head + 1, cols], 100.0)
                    mixed = (score_ref[rows, cols] * jnp.exp2(gap)).astype(BF16)
                    total = total + jnp.dot(mixed, u[cols], preferred_element_type=F32)
                pieces.append(total)
            lane = lax.broadcasted_iota(jnp.int32, (TILE, 128), 1)
            y = jnp.where(lane < HEAD_DIM, pieces[0], pieces[1])
            y_ref[rows, lanes] = (y + skip_ref[:, lanes] * u[rows].astype(F32)).astype(BF16)


def norm_kernel(y_ref, gate_ref, state_ref, read_ref, enter_ref, gain_ref, out_ref, held_ref):
    rows, width = y_ref.shape
    heads = width // HEAD_DIM
    enter = enter_ref[0]
    square = jnp.zeros((rows, 256), F32)
    for at in range(0, width, 256):
        lanes = slice(at, at + 256)
        carried = lax.dot_general(
            read_ref[...], state_ref[lanes, :], (((1,), (1,)), ((), ())), preferred_element_type=F32
        )
        factor = jnp.dot(
            enter, spread_matrix(2 * heads, 256, at // HEAD_DIM, heads), preferred_element_type=F32
        )
        y = y_ref[:, lanes].astype(F32) + carried * factor
        gated = y * silu(gate_ref[:, lanes].astype(F32))
        square = square + gated * gated
        held_ref[:, lanes] = gated
    mean = jnp.sum(square, axis=1, keepdims=True) * (1.0 / width)
    scale = lax.rsqrt(mean + EPSILON)
    for at in range(0, width, 256):
        lanes = slice(at, at + 256)
        out_ref[:, lanes] = (held_ref[:, lanes] * scale * gain_ref[:, lanes]).astype(BF16)


def split_high_low(values):
    high = lax.reduce_precision(values, 8, 7)
    return jnp.concatenate([high, values - high], axis=-1).astype(BF16)


def per_device(
    inner_input,
    state_input,
    gate_input,
    inner_taps,
    inner_bias,
    state_taps,
    state_bias,
    step_raw,
    step_bias,
    decay_log,
    skip_gain,
    norm_gain,
    out_weight,
    sequence_lengths,
):
    tokens, inner_width = inner_input.shape
    heads = step_raw.shape[0]
    groups = state_input.shape[1] // (2 * STATE_DIM)
    per_group = heads // groups
    group_width = per_group * HEAD_DIM
    seq_count = lax.axis_size("seq")
    head_count = lax.axis_size("head")
    rows_count = seq_count // 2
    seq_at = lax.axis_index("seq")
    head_at = lax.axis_index("head")
    row_at, side = seq_at // 2, seq_at % 2

    def swapped(value):
        return lax.ppermute(value, "seq", [(s, s ^ 1) for s in range(seq_count)])

    def moved(value, by):
        pairs = [(s, s + by) for s in range(seq_count) if 0 <= s + by < seq_count]
        return lax.ppermute(value, "seq", pairs)

    up, down = [out_weight], [out_weight]
    for _ in range(rows_count - 1):
        up.append(moved(up[-1], 2))
        down.append(moved(down[-1], -2))

    halo = moved(
        jnp.concatenate([inner_input[tokens - HALO :], state_input[tokens - HALO :]], axis=1), 1
    )
    positions = seq_at * tokens + lax.iota(jnp.int32, tokens + 3) - 3
    seg_extended = segment_of(positions, sequence_lengths)
    seg = seg_extended[3:]
    masks = jnp.stack(
        [(seg_extended[3 - k : 3 - k + tokens] == seg) for k in (1, 2, 3)] + [seg < 0] * 5, axis=1
    ).astype(F32)
    steps = jax.nn.softplus(step_raw + step_bias[:, None])
    running = jnp.cumsum(-jnp.exp(decay_log)[:, None] * steps, axis=1)
    running = running - SEGMENT_DROP * (seg - seg_extended[2]).astype(F32)[None, :]
    last = running[:, tokens - 1 :]
    closing = jnp.exp(last - running) * steps
    entering = jnp.exp(running)
    factor = jnp.exp(last[:, 0])
    shape = (heads // STEP_HEADS, STEP_HEADS, tokens)
    col_log = jnp.transpose((running * LOG2E).reshape(shape), (0, 2, 1))
    row_log = (running - jnp.log(steps)) * LOG2E
    close = split_high_low(jnp.transpose(closing.reshape(shape), (0, 2, 1)))
    enter = split_high_low(
        jnp.transpose(entering.reshape(groups, per_group, tokens), (0, 2, 1))
    )

    width = STEP_HEADS * HEAD_DIM
    per_steps = per_group // STEP_HEADS
    pair_width = 2 * STATE_DIM
    step_cols = lambda i: (0, i)
    group_cols = lambda i: (0, i // per_steps)
    y_local, end_state, read_all = pl.pallas_call(
        partial(local_kernel, per_steps),
        grid=(heads // STEP_HEADS,),
        in_specs=[
            pl.BlockSpec((tokens, width), step_cols),
            pl.BlockSpec((HALO, width), step_cols),
            pl.BlockSpec((4, width), step_cols),
            pl.BlockSpec((1, width), step_cols),
            pl.BlockSpec((tokens, pair_width), group_cols),
            pl.BlockSpec((HALO, pair_width), group_cols),
            pl.BlockSpec((4, pair_width), group_cols),
            pl.BlockSpec((1, pair_width), group_cols),
            pl.BlockSpec((tokens, 8), lambda i: (0, 0)),
            pl.BlockSpec((1, tokens, STEP_HEADS), lambda i: (i, 0, 0)),
            pl.BlockSpec((STEP_HEADS, tokens), lambda i: (i, 0)),
            pl.BlockSpec((1, tokens, 2 * STEP_HEADS), lambda i: (i, 0, 0)),
            pl.BlockSpec((1, width), step_cols),
        ],
        out_specs=[
            pl.BlockSpec((tokens, width), step_cols),
            pl.BlockSpec((width, STATE_DIM), lambda i: (i, 0)),
            pl.BlockSpec((tokens, STATE_DIM), group_cols),
        ],
        out_shape=[
            jax.ShapeDtypeStruct((tokens, inner_width), BF16),
            jax.ShapeDtypeStruct((inner_width, STATE_DIM), BF16),
            jax.ShapeDtypeStruct((tokens, groups * STATE_DIM), BF16),
        ],
        scratch_shapes=[
            pltpu.VMEM((tokens, tokens), F32),
            pltpu.VMEM((tokens, STATE_DIM), BF16),
        ],
        compiler_params=pltpu.CompilerParams(vmem_limit_bytes=32 * 2**20),
        cost_estimate=pl.CostEstimate(
            flops=20 * 10**9, bytes_accessed=16 * 2**20, transcendentals=12 * 10**6
        ),
        name="local_scan",
    )(
        inner_input,
        halo[:, :inner_width],
        inner_taps.astype(F32),
        inner_bias.astype(F32)[None],
        state_input,
        halo[:, inner_width:],
        state_taps.astype(F32),
        state_bias.astype(F32)[None],
        masks,
        col_log,
        row_log,
        close,
        jnp.repeat(skip_gain, HEAD_DIM)[None],
    )

    half = heads // 2
    half_rows = half * HEAD_DIM

    def half_of(value, which):
        return lax.dynamic_slice_in_dim(value, which * (value.shape[0] // 2), value.shape[0] // 2)

    def per_row(value):
        return jnp.repeat(value, HEAD_DIM)[:, None]

    factor_other = swapped(factor)
    mine, other = half_of(end_state, side), half_of(end_state, 1 - side)
    peer_end = swapped(other).astype(F32)
    mine = mine.astype(F32)
    first_end = jnp.where(side == 0, mine, peer_end)
    second_end = jnp.where(side == 0, peer_end, mine)
    first_factor = per_row(half_of(jnp.where(side == 0, factor, factor_other), side))
    second_factor = per_row(half_of(jnp.where(side == 0, factor_other, factor), side))
    pair_total = second_factor * first_end + second_end
    pair_factor = first_factor * second_factor
    window = pair_total
    for hop in range(max(1, seq_count // 4)):
        arriving = moved(window.astype(BF16), 2).astype(F32)
        window = pair_total + pair_factor * arriving
    after_first = (first_factor * arriving + first_end).astype(BF16)
    arriving = arriving.astype(BF16)
    own_part = jnp.where(side == 0, arriving, after_first)
    peer_part = swapped(jnp.where(side == 0, after_first, arriving))
    state_low = jnp.where(side == 0, own_part, peer_part)
    state_high = jnp.where(side == 0, peer_part, own_part)
    state_in = jnp.concatenate([state_low, state_high], axis=0)

    gains = norm_gain.astype(F32)[None]
    own, peer = [], []
    for group in range(groups):
        normed = pl.pallas_call(
            norm_kernel,
            grid=(tokens // TILE,),
            in_specs=[
                pl.BlockSpec((TILE, group_width), lambda i, g=group: (i, g)),
                pl.BlockSpec((TILE, group_width), lambda i, g=group: (i, g)),
                pl.BlockSpec((group_width, STATE_DIM), lambda i, g=group: (g, 0)),
                pl.BlockSpec((TILE, STATE_DIM), lambda i, g=group: (i, g)),
                pl.BlockSpec((1, TILE, 2 * per_group), lambda i, g=group: (g, i, 0)),
                pl.BlockSpec((1, group_width), lambda i, g=group: (0, g)),
            ],
            out_specs=pl.BlockSpec((TILE, group_width), lambda i: (i, 0)),
            out_shape=jax.ShapeDtypeStruct((tokens, group_width), BF16),
            scratch_shapes=[pltpu.VMEM((TILE, group_width), F32)],
            compiler_params=pltpu.CompilerParams(vmem_limit_bytes=32 * 2**20),
            cost_estimate=pl.CostEstimate(
                flops=10**9, bytes_accessed=8 * 2**20, transcendentals=10**6
            ),
            name="gated_norm",
        )(y_local, gate_input, state_in, read_all, enter, gains)
        own.append(normed)
        peer.append(swapped(normed))
    own = jnp.concatenate(own, axis=1)
    peer = jnp.concatenate(peer, axis=1)
    acts = jnp.concatenate([own, peer], axis=0)

    partials = []
    for distance in range(rows_count):
        if distance == 0:
            weight = out_weight
        else:
            weight = jnp.where(row_at >= distance, up[distance], down[rows_count - distance])
        partials.append(jnp.dot(acts, weight, preferred_element_type=F32).astype(BF16))
    stacked = jnp.stack(partials)
    ordered = [
        lax.dynamic_index_in_dim(stacked, (row_at - at) % rows_count, 0, False)
        for at in range(rows_count)
    ]
    per_head = rows_count // head_count
    blocks = jnp.stack(ordered).reshape(head_count, per_head, *partials[0].shape)
    bit = 1
    while bit < head_count:
        high = blocks.shape[0] // 2
        split = blocks.reshape(high, 2, *blocks.shape[1:])
        mine_bit = (head_at // bit) % 2
        keep = lax.dynamic_index_in_dim(split, mine_bit, 1, False)
        send = lax.dynamic_index_in_dim(split, 1 - mine_bit, 1, False)
        got = lax.ppermute(send, "head", [(h, h ^ bit) for h in range(head_count)])
        blocks = (keep.astype(F32) + got.astype(F32)).astype(BF16)
        bit *= 2
    final = blocks[0]
    mine_out = final[:, :tokens]
    peer_out = swapped(final[:, tokens:])
    even = jnp.where(side == 0, mine_out, peer_out)
    odd = jnp.where(side == 0, peer_out, mine_out)
    both = jnp.stack([even, odd], axis=1)
    return jnp.transpose(both, (2, 0, 1, 3)).reshape(tokens, -1)


def solution(mesh):
    in_specs = (
        P("seq", "head"),
        P("seq", "head"),
        P("seq", "head"),
        P(None, "head"),
        P("head"),
        P(None, "head"),
        P("head"),
        P("head", "seq"),
        P("head"),
        P("head"),
        P("head"),
        P("head"),
        P("head", "seq"),
        P(),
    )
    out_specs = P("seq", "head")
    return jax.shard_map(
        per_device, mesh=mesh, in_specs=in_specs, out_specs=out_specs, check_vma=False
    )
```

```python
from functools import partial

import jax
import jax.numpy as jnp
from jax import lax
from jax.experimental import pallas as pl
from jax.experimental.pallas import tpu as pltpu
from jax.sharding import PartitionSpec as P

HEAD_DIM = 64
STATE_DIM = 256
HALO = 16
TILE = 256
STEP_HEADS = 8
LOG2E = 1.4426950408889634
SEGMENT_DROP = 200.0
EPSILON = 1e-05
BF16 = jnp.bfloat16
F32 = jnp.float32


def segment_of(positions, sequence_lengths):
    starts = jnp.cumsum(sequence_lengths) - sequence_lengths
    hits = (positions[:, None] >= starts[None, :]).astype(jnp.int32)
    return jnp.sum(hits, axis=1) - 1


def silu(v):
    return v * (0.5 * jnp.tanh(0.5 * v) + 0.5)


def conv(values, halo, masks, taps, bias):
    now = values.astype(F32)
    extended = jnp.concatenate([halo.astype(F32), now], axis=0)
    total = bias + taps[3:4] * now
    for back in range(1, 4):
        shifted = pltpu.roll(extended, back, 0)[HALO:]
        total = total + taps[3 - back : 4 - back] * (shifted * masks[:, back - 1 : back])
    return silu(total).astype(BF16)


def spread_matrix(rows, width, first_head, heads):
    row = lax.broadcasted_iota(jnp.int32, (rows, width), 0)
    col = lax.broadcasted_iota(jnp.int32, (rows, width), 1)
    return (row % heads == first_head + col // HEAD_DIM).astype(F32).astype(BF16)


def local_kernel(
    per_group_steps,
    x_ref,
    xh_ref,
    xt_ref,
    xb_ref,
    s_ref,
    sh_ref,
    st_ref,
    sb_ref,
    mask_ref,
    col_ref,
    row_ref,
    close_ref,
    skip_ref,
    y_ref,
    end_ref,
    read_ref,
    score_ref,
    write_ref,
):
    tokens = x_ref.shape[0]

    @pl.when(pl.program_id(0) % per_group_steps == 0)
    def _():
        masks = mask_ref[...]
        for part in range(2 * STATE_DIM // 128):
            lanes = slice(part * 128, part * 128 + 128)
            vec = conv(
                s_ref[:, lanes], sh_ref[:, lanes], masks, st_ref[:, lanes], sb_ref[:, lanes]
            )
            if part * 128 < STATE_DIM:
                write_ref[:, lanes] = vec
            else:
                read_ref[:, part * 128 - STATE_DIM : part * 128 - STATE_DIM + 128] = vec
        for at in range(0, tokens, TILE):
            score = lax.dot_general(
                read_ref[at : at + TILE, :],
                write_ref[: at + TILE, :],
                (((1,), (1,)), ((), ())),
                preferred_element_type=F32,
            )
            row = lax.broadcasted_iota(jnp.int32, score.shape, 0) + at
            col = lax.broadcasted_iota(jnp.int32, score.shape, 1)
            score_ref[at : at + TILE, : at + TILE] = jnp.where(row >= col, score, 0.0)

    masks = mask_ref[...]
    close = close_ref[0]
    for pair in range(STEP_HEADS // 2):
        lanes = slice(pair * 128, pair * 128 + 128)
        u = conv(x_ref[:, lanes], xh_ref[:, lanes], masks, xt_ref[:, lanes], xb_ref[:, lanes])
        weight = jnp.dot(
            close,
            spread_matrix(2 * STEP_HEADS, 128, 2 * pair, STEP_HEADS),
            preferred_element_type=F32,
        )
        weighted = (u.astype(F32) * weight).astype(BF16)
        end_ref[lanes, :] = lax.dot_general(
            weighted, write_ref[...], (((0,), (0,)), ((), ())), preferred_element_type=F32
        ).astype(BF16)
        for at in range(0, tokens, TILE):
            rows = slice(at, at + TILE)
            pieces = []
            for head in (2 * pair, 2 * pair + 1):
                here = col_ref[0, rows, head : head + 1]
                total = jnp.zeros((TILE, 128), F32)
                for back in range(0, at + TILE, TILE):
                    cols = slice(back, back + TILE)
                    gap = jnp.minimum(here - row_ref[head : head + 1, cols], 100.0)
                    mixed = (score_ref[rows, cols] * jnp.exp2(gap)).astype(BF16)
                    total = total + jnp.dot(mixed, u[cols], preferred_element_type=F32)
                pieces.append(total)
            lane = lax.broadcasted_iota(jnp.int32, (TILE, 128), 1)
            y = jnp.where(lane < HEAD_DIM, pieces[0], pieces[1])
            y_ref[rows, lanes] = (y + skip_ref[:, lanes] * u[rows].astype(F32)).astype(BF16)


def norm_kernel(y_ref, gate_ref, state_ref, read_ref, enter_ref, gain_ref, out_ref, held_ref):
    rows, width = y_ref.shape
    heads = width // HEAD_DIM
    enter = enter_ref[0]
    square = jnp.zeros((rows, 256), F32)
    for at in range(0, width, 256):
        lanes = slice(at, at + 256)
        carried = lax.dot_general(
            read_ref[...], state_ref[lanes, :], (((1,), (1,)), ((), ())), preferred_element_type=F32
        )
        factor = jnp.dot(
            enter, spread_matrix(2 * heads, 256, at // HEAD_DIM, heads), preferred_element_type=F32
        )
        y = y_ref[:, lanes].astype(F32) + carried * factor
        gated = y * silu(gate_ref[:, lanes].astype(F32))
        square = square + gated * gated
        held_ref[:, lanes] = gated
    mean = jnp.sum(square, axis=1, keepdims=True) * (1.0 / width)
    scale = lax.rsqrt(mean + EPSILON)
    for at in range(0, width, 256):
        lanes = slice(at, at + 256)
        out_ref[:, lanes] = (held_ref[:, lanes] * scale * gain_ref[:, lanes]).astype(BF16)


def project_kernel(depth, first_ref, *refs):
    acts, (one_ref, two_ref, out_ref) = refs[:-3], refs[-3:]
    tokens, width = acts[0].shape
    parts = depth // width

    def multiply(weight_ref):
        for half in range(2):
            total = jnp.zeros((tokens, weight_ref.shape[1]), F32)
            for part in range(parts):
                total = total + jnp.dot(
                    acts[half * parts + part][...],
                    weight_ref[part * width : part * width + width, :],
                    preferred_element_type=F32,
                )
            out_ref[half * tokens : half * tokens + tokens, :] = total.astype(BF16)

    @pl.when(first_ref[0] == 1)
    def _():
        multiply(one_ref)

    @pl.when(first_ref[0] != 1)
    def _():
        multiply(two_ref)


def project(acts, one, two, first):
    tokens, width = acts[0].shape
    depth, features = one.shape
    tile = min(features, 256)
    whole = pl.BlockSpec((tokens, width), lambda i, f: (0, 0))
    return pl.pallas_call(
        partial(project_kernel, depth),
        grid_spec=pltpu.PrefetchScalarGridSpec(
            num_scalar_prefetch=1,
            grid=(features // tile,),
            in_specs=[whole] * len(acts)
            + [
                pl.BlockSpec((depth, tile), lambda i, f: (0, i * f[0])),
                pl.BlockSpec((depth, tile), lambda i, f: (0, i * (1 - f[0]))),
            ],
            out_specs=pl.BlockSpec((2 * tokens, tile), lambda i, f: (0, i)),
        ),
        out_shape=jax.ShapeDtypeStruct((2 * tokens, features), BF16),
        compiler_params=pltpu.CompilerParams(vmem_limit_bytes=48 * 2**20),
        cost_estimate=pl.CostEstimate(flops=10**6, bytes_accessed=10**6, transcendentals=0),
        name="project",
    )(first, *acts, one, two)


def split_high_low(values):
    high = lax.reduce_precision(values, 8, 7)
    return jnp.concatenate([high, values - high], axis=-1).astype(BF16)


def per_device(
    inner_input,
    state_input,
    gate_input,
    inner_taps,
    inner_bias,
    state_taps,
    state_bias,
    step_raw,
    step_bias,
    decay_log,
    skip_gain,
    norm_gain,
    out_weight,
    sequence_lengths,
):
    tokens, inner_width = inner_input.shape
    heads = step_raw.shape[0]
    groups = state_input.shape[1] // (2 * STATE_DIM)
    per_group = heads // groups
    group_width = per_group * HEAD_DIM
    seq_count = lax.axis_size("seq")
    head_count = lax.axis_size("head")
    rows_count = seq_count // 2
    seq_at = lax.axis_index("seq")
    head_at = lax.axis_index("head")
    row_at, side = seq_at // 2, seq_at % 2

    def swapped(value):
        return lax.ppermute(value, "seq", [(s, s ^ 1) for s in range(seq_count)])

    def moved(value, by):
        pairs = [(s, s + by) for s in range(seq_count) if 0 <= s + by < seq_count]
        return lax.ppermute(value, "seq", pairs)

    up, down = [out_weight], [out_weight]
    for _ in range(rows_count - 1):
        up.append(moved(up[-1], 2))
        down.append(moved(down[-1], -2))

    halo = moved(
        jnp.concatenate([inner_input[tokens - HALO :], state_input[tokens - HALO :]], axis=1), 1
    )
    positions = seq_at * tokens + lax.iota(jnp.int32, tokens + 3) - 3
    seg_extended = segment_of(positions, sequence_lengths)
    seg = seg_extended[3:]
    masks = jnp.stack(
        [(seg_extended[3 - k : 3 - k + tokens] == seg) for k in (1, 2, 3)] + [seg < 0] * 5, axis=1
    ).astype(F32)
    steps = jax.nn.softplus(step_raw + step_bias[:, None])
    running = jnp.cumsum(-jnp.exp(decay_log)[:, None] * steps, axis=1)
    running = running - SEGMENT_DROP * (seg - seg_extended[2]).astype(F32)[None, :]
    last = running[:, tokens - 1 :]
    closing = jnp.exp(last - running) * steps
    entering = jnp.exp(running)
    factor = jnp.exp(last[:, 0])
    shape = (heads // STEP_HEADS, STEP_HEADS, tokens)
    col_log = jnp.transpose((running * LOG2E).reshape(shape), (0, 2, 1))
    row_log = (running - jnp.log(steps)) * LOG2E
    close = split_high_low(jnp.transpose(closing.reshape(shape), (0, 2, 1)))
    enter = split_high_low(
        jnp.transpose(entering.reshape(groups, per_group, tokens), (0, 2, 1))
    )

    width = STEP_HEADS * HEAD_DIM
    per_steps = per_group // STEP_HEADS
    pair_width = 2 * STATE_DIM
    step_cols = lambda i: (0, i)
    group_cols = lambda i: (0, i // per_steps)
    y_local, end_state, read_all = pl.pallas_call(
        partial(local_kernel, per_steps),
        grid=(heads // STEP_HEADS,),
        in_specs=[
            pl.BlockSpec((tokens, width), step_cols),
            pl.BlockSpec((HALO, width), step_cols),
            pl.BlockSpec((4, width), step_cols),
            pl.BlockSpec((1, width), step_cols),
            pl.BlockSpec((tokens, pair_width), group_cols),
            pl.BlockSpec((HALO, pair_width), group_cols),
            pl.BlockSpec((4, pair_width), group_cols),
            pl.BlockSpec((1, pair_width), group_cols),
            pl.BlockSpec((tokens, 8), lambda i: (0, 0)),
            pl.BlockSpec((1, tokens, STEP_HEADS), lambda i: (i, 0, 0)),
            pl.BlockSpec((STEP_HEADS, tokens), lambda i: (i, 0)),
            pl.BlockSpec((1, tokens, 2 * STEP_HEADS), lambda i: (i, 0, 0)),
            pl.BlockSpec((1, width), step_cols),
        ],
        out_specs=[
            pl.BlockSpec((tokens, width), step_cols),
            pl.BlockSpec((width, STATE_DIM), lambda i: (i, 0)),
            pl.BlockSpec((tokens, STATE_DIM), group_cols),
        ],
        out_shape=[
            jax.ShapeDtypeStruct((tokens, inner_width), BF16),
            jax.ShapeDtypeStruct((inner_width, STATE_DIM), BF16),
            jax.ShapeDtypeStruct((tokens, groups * STATE_DIM), BF16),
        ],
        scratch_shapes=[
            pltpu.VMEM((tokens, tokens), F32),
            pltpu.VMEM((tokens, STATE_DIM), BF16),
        ],
        compiler_params=pltpu.CompilerParams(vmem_limit_bytes=32 * 2**20),
        cost_estimate=pl.CostEstimate(
            flops=10**6, bytes_accessed=10**6, transcendentals=0
        ),
        name="local_scan",
    )(
        inner_input,
        halo[:, :inner_width],
        inner_taps.astype(F32),
        inner_bias.astype(F32)[None],
        state_input,
        halo[:, inner_width:],
        state_taps.astype(F32),
        state_bias.astype(F32)[None],
        masks,
        col_log,
        row_log,
        close,
        jnp.repeat(skip_gain, HEAD_DIM)[None],
    )

    half = heads // 2
    half_rows = half * HEAD_DIM

    def half_of(value, which):
        return lax.dynamic_slice_in_dim(value, which * (value.shape[0] // 2), value.shape[0] // 2)

    def per_row(value):
        return jnp.repeat(value, HEAD_DIM)[:, None]

    factor_other = swapped(factor)
    mine, other = half_of(end_state, side), half_of(end_state, 1 - side)
    peer_end = swapped(other).astype(F32)
    mine = mine.astype(F32)
    first_end = jnp.where(side == 0, mine, peer_end)
    second_end = jnp.where(side == 0, peer_end, mine)
    first_factor = per_row(half_of(jnp.where(side == 0, factor, factor_other), side))
    second_factor = per_row(half_of(jnp.where(side == 0, factor_other, factor), side))
    pair_total = second_factor * first_end + second_end
    pair_factor = first_factor * second_factor
    window = pair_total
    for hop in range(max(1, seq_count // 4)):
        arriving = moved(window.astype(BF16), 2).astype(F32)
        window = pair_total + pair_factor * arriving
    after_first = (first_factor * arriving + first_end).astype(BF16)
    arriving = arriving.astype(BF16)
    own_part = jnp.where(side == 0, arriving, after_first)
    peer_part = swapped(jnp.where(side == 0, after_first, arriving))
    state_low = jnp.where(side == 0, own_part, peer_part)
    state_high = jnp.where(side == 0, peer_part, own_part)
    state_in = jnp.concatenate([state_low, state_high], axis=0)

    gains = norm_gain.astype(F32)[None]
    own, peer = [], []
    for group in range(groups):
        normed = pl.pallas_call(
            norm_kernel,
            grid=(tokens // TILE,),
            in_specs=[
                pl.BlockSpec((TILE, group_width), lambda i, g=group: (i, g)),
                pl.BlockSpec((TILE, group_width), lambda i, g=group: (i, g)),
                pl.BlockSpec((group_width, STATE_DIM), lambda i, g=group: (g, 0)),
                pl.BlockSpec((TILE, STATE_DIM), lambda i, g=group: (i, g)),
                pl.BlockSpec((1, TILE, 2 * per_group), lambda i, g=group: (g, i, 0)),
                pl.BlockSpec((1, group_width), lambda i, g=group: (0, g)),
            ],
            out_specs=pl.BlockSpec((TILE, group_width), lambda i: (i, 0)),
            out_shape=jax.ShapeDtypeStruct((tokens, group_width), BF16),
            scratch_shapes=[pltpu.VMEM((TILE, group_width), F32)],
            compiler_params=pltpu.CompilerParams(vmem_limit_bytes=32 * 2**20),
            cost_estimate=pl.CostEstimate(
                flops=10**6, bytes_accessed=10**6, transcendentals=0
            ),
            name="gated_norm",
        )(y_local, gate_input, state_in, read_all, enter, gains)
        own.append(normed)
        peer.append(swapped(normed))
    acts = own + peer

    per_head = rows_count // head_count
    reduced = []
    for distance in range(rows_count):
        if distance == 0:
            one, two, first = out_weight, out_weight, jnp.ones((1,), jnp.int32)
        else:
            one, two = up[distance], down[rows_count - distance]
            first = (row_at >= distance).astype(jnp.int32)[None]
        value = project(acts, one, two, first)
        bit = 1
        while bit < head_count:
            pairs = []
            for s in range(seq_count):
                owner = (s // 2 - distance) % rows_count // per_head
                for h in range(head_count):
                    if h % bit == owner % bit and (h ^ owner) & bit:
                        pairs.append((s * head_count + h, s * head_count + (h ^ bit)))
            got = lax.ppermute(value, ("seq", "head"), pairs)
            value = (value.astype(F32) + got.astype(F32)).astype(BF16)
            bit *= 2
        reduced.append(value)
    finals = []
    for shard in range(per_head):
        wanted = (row_at - head_at * per_head - shard) % rows_count
        chosen = reduced[0]
        for distance in range(1, rows_count):
            chosen = jnp.where(wanted == distance, reduced[distance], chosen)
        finals.append(chosen)
    final = jnp.stack(finals)
    mine_out = final[:, :tokens]
    peer_out = swapped(final[:, tokens:])
    even = jnp.where(side == 0, mine_out, peer_out)
    odd = jnp.where(side == 0, peer_out, mine_out)
    both = jnp.stack([even, odd], axis=1)
    return jnp.transpose(both, (2, 0, 1, 3)).reshape(tokens, -1)


def solution(mesh):
    in_specs = (
        P("seq", "head"),
        P("seq", "head"),
        P("seq", "head"),
        P(None, "head"),
        P("head"),
        P(None, "head"),
        P("head"),
        P("head", "seq"),
        P("head"),
        P("head"),
        P("head"),
        P("head"),
        P("head", "seq"),
        P(),
    )
    out_specs = P("seq", "head")
    return jax.shard_map(
        per_device, mesh=mesh, in_specs=in_specs, out_specs=out_specs, check_vma=False
    )
```

```python
from functools import partial

import jax
import jax.numpy as jnp
from jax import lax
from jax.experimental import pallas as pl
from jax.experimental.pallas import tpu as pltpu
from jax.sharding import PartitionSpec as P

HEAD_DIM = 64
STATE_DIM = 256
HALO = 16
TILE = 256
STEP_HEADS = 8
LOG2E = 1.4426950408889634
SEGMENT_DROP = 200.0
EPSILON = 1e-05
BF16 = jnp.bfloat16
F32 = jnp.float32


def segment_of(positions, sequence_lengths):
    starts = jnp.cumsum(sequence_lengths) - sequence_lengths
    hits = (positions[:, None] >= starts[None, :]).astype(jnp.int32)
    return jnp.sum(hits, axis=1) - 1


def silu(v):
    return v * (0.5 * jnp.tanh(0.5 * v) + 0.5)


def conv(values, halo, masks, taps, bias):
    now = values.astype(F32)
    extended = jnp.concatenate([halo.astype(F32), now], axis=0)
    total = bias + taps[3:4] * now
    for back in range(1, 4):
        shifted = pltpu.roll(extended, back, 0)[HALO:]
        total = total + taps[3 - back : 4 - back] * (shifted * masks[:, back - 1 : back])
    return silu(total).astype(BF16)


def spread_matrix(rows, width, first_head, heads):
    row = lax.broadcasted_iota(jnp.int32, (rows, width), 0)
    col = lax.broadcasted_iota(jnp.int32, (rows, width), 1)
    return (row % heads == first_head + col // HEAD_DIM).astype(F32).astype(BF16)


def local_kernel(
    per_group_steps,
    x_ref,
    xh_ref,
    xt_ref,
    xb_ref,
    s_ref,
    sh_ref,
    st_ref,
    sb_ref,
    mask_ref,
    col_ref,
    row_ref,
    close_ref,
    skip_ref,
    y_ref,
    end_ref,
    read_ref,
    score_ref,
    write_ref,
):
    tokens = x_ref.shape[0]

    @pl.when(pl.program_id(0) % per_group_steps == 0)
    def _():
        masks = mask_ref[...]
        for part in range(2 * STATE_DIM // 128):
            lanes = slice(part * 128, part * 128 + 128)
            vec = conv(
                s_ref[:, lanes], sh_ref[:, lanes], masks, st_ref[:, lanes], sb_ref[:, lanes]
            )
            if part * 128 < STATE_DIM:
                write_ref[:, lanes] = vec
            else:
                read_ref[:, part * 128 - STATE_DIM : part * 128 - STATE_DIM + 128] = vec
        for at in range(0, tokens, TILE):
            score = lax.dot_general(
                read_ref[at : at + TILE, :],
                write_ref[: at + TILE, :],
                (((1,), (1,)), ((), ())),
                preferred_element_type=F32,
            )
            row = lax.broadcasted_iota(jnp.int32, score.shape, 0) + at
            col = lax.broadcasted_iota(jnp.int32, score.shape, 1)
            score_ref[at : at + TILE, : at + TILE] = jnp.where(row >= col, score, 0.0)

    masks = mask_ref[...]
    close = close_ref[0]
    for pair in range(STEP_HEADS // 2):
        lanes = slice(pair * 128, pair * 128 + 128)
        u = conv(x_ref[:, lanes], xh_ref[:, lanes], masks, xt_ref[:, lanes], xb_ref[:, lanes])
        weight = jnp.dot(
            close,
            spread_matrix(2 * STEP_HEADS, 128, 2 * pair, STEP_HEADS),
            preferred_element_type=F32,
        )
        weighted = (u.astype(F32) * weight).astype(BF16)
        end_ref[lanes, :] = lax.dot_general(
            weighted, write_ref[...], (((0,), (0,)), ((), ())), preferred_element_type=F32
        ).astype(BF16)
        for at in range(0, tokens, TILE):
            rows = slice(at, at + TILE)
            pieces = []
            for head in (2 * pair, 2 * pair + 1):
                here = col_ref[0, rows, head : head + 1]
                total = jnp.zeros((TILE, 128), F32)
                for back in range(0, at + TILE, TILE):
                    cols = slice(back, back + TILE)
                    gap = jnp.minimum(here - row_ref[head : head + 1, cols], 100.0)
                    mixed = (score_ref[rows, cols] * jnp.exp2(gap)).astype(BF16)
                    total = total + jnp.dot(mixed, u[cols], preferred_element_type=F32)
                pieces.append(total)
            lane = lax.broadcasted_iota(jnp.int32, (TILE, 128), 1)
            y = jnp.where(lane < HEAD_DIM, pieces[0], pieces[1])
            y_ref[rows, lanes] = (y + skip_ref[:, lanes] * u[rows].astype(F32)).astype(BF16)


def norm_kernel(y_ref, gate_ref, state_ref, read_ref, enter_ref, gain_ref, out_ref, held_ref):
    rows, width = y_ref.shape
    heads = width // HEAD_DIM
    enter = enter_ref[0]
    square = jnp.zeros((rows, 256), F32)
    for at in range(0, width, 256):
        lanes = slice(at, at + 256)
        carried = lax.dot_general(
            read_ref[...], state_ref[lanes, :], (((1,), (1,)), ((), ())), preferred_element_type=F32
        )
        factor = jnp.dot(
            enter, spread_matrix(2 * heads, 256, at // HEAD_DIM, heads), preferred_element_type=F32
        )
        y = y_ref[:, lanes].astype(F32) + carried * factor
        gated = y * silu(gate_ref[:, lanes].astype(F32))
        square = square + gated * gated
        held_ref[:, lanes] = gated
    mean = jnp.sum(square, axis=1, keepdims=True) * (1.0 / width)
    scale = lax.rsqrt(mean + EPSILON)
    for at in range(0, width, 256):
        lanes = slice(at, at + 256)
        out_ref[:, lanes] = (held_ref[:, lanes] * scale * gain_ref[:, lanes]).astype(BF16)


def project_kernel(depth, first_ref, *refs):
    acts, (one_ref, two_ref, out_ref) = refs[:-3], refs[-3:]
    tokens, width = acts[0].shape
    parts = depth // width

    def multiply(weight_ref):
        for half in range(2):
            total = jnp.zeros((tokens, weight_ref.shape[1]), F32)
            for part in range(parts):
                total = total + jnp.dot(
                    acts[half * parts + part][...],
                    weight_ref[part * width : part * width + width, :],
                    preferred_element_type=F32,
                )
            out_ref[half * tokens : half * tokens + tokens, :] = total.astype(BF16)

    @pl.when(first_ref[0] == 1)
    def _():
        multiply(one_ref)

    @pl.when(first_ref[0] != 1)
    def _():
        multiply(two_ref)


def project(acts, one, two, first):
    tokens, width = acts[0].shape
    depth, features = one.shape
    tile = min(features, 256)
    whole = pl.BlockSpec((tokens, width), lambda i, f: (0, 0))
    return pl.pallas_call(
        partial(project_kernel, depth),
        grid_spec=pltpu.PrefetchScalarGridSpec(
            num_scalar_prefetch=1,
            grid=(features // tile,),
            in_specs=[whole] * len(acts)
            + [
                pl.BlockSpec((depth, tile), lambda i, f: (0, i * f[0])),
                pl.BlockSpec((depth, tile), lambda i, f: (0, i * (1 - f[0]))),
            ],
            out_specs=pl.BlockSpec((2 * tokens, tile), lambda i, f: (0, i)),
        ),
        out_shape=jax.ShapeDtypeStruct((2 * tokens, features), BF16),
        compiler_params=pltpu.CompilerParams(vmem_limit_bytes=48 * 2**20),
        cost_estimate=pl.CostEstimate(flops=10**6, bytes_accessed=10**6, transcendentals=0),
        name="project",
    )(first, *acts, one, two)


def split_high_low(values):
    high = lax.reduce_precision(values, 8, 7)
    return jnp.concatenate([high, values - high], axis=-1).astype(BF16)


def per_device(
    inner_input,
    state_input,
    gate_input,
    inner_taps,
    inner_bias,
    state_taps,
    state_bias,
    step_raw,
    step_bias,
    decay_log,
    skip_gain,
    norm_gain,
    out_weight,
    sequence_lengths,
):
    tokens, inner_width = inner_input.shape
    heads = step_raw.shape[0]
    groups = state_input.shape[1] // (2 * STATE_DIM)
    per_group = heads // groups
    group_width = per_group * HEAD_DIM
    seq_count = lax.axis_size("seq")
    head_count = lax.axis_size("head")
    rows_count = seq_count // 2
    seq_at = lax.axis_index("seq")
    head_at = lax.axis_index("head")
    row_at, side = seq_at // 2, seq_at % 2

    def swapped(value):
        return lax.ppermute(value, "seq", [(s, s ^ 1) for s in range(seq_count)])

    def moved(value, by):
        pairs = [(s, s + by) for s in range(seq_count) if 0 <= s + by < seq_count]
        return lax.ppermute(value, "seq", pairs)

    halo = moved(
        jnp.concatenate([inner_input[tokens - HALO :], state_input[tokens - HALO :]], axis=1), 1
    )
    first_weight, halo = lax.optimization_barrier((out_weight, halo))
    up, down = [out_weight], [out_weight]
    if rows_count > 1:
        up.append(moved(first_weight, 2))
        down.append(moved(first_weight, -2))
    positions = seq_at * tokens + lax.iota(jnp.int32, tokens + 3) - 3
    seg_extended = segment_of(positions, sequence_lengths)
    seg = seg_extended[3:]
    masks = jnp.stack(
        [(seg_extended[3 - k : 3 - k + tokens] == seg) for k in (1, 2, 3)] + [seg < 0] * 5, axis=1
    ).astype(F32)
    steps = jax.nn.softplus(step_raw + step_bias[:, None])
    running = jnp.cumsum(-jnp.exp(decay_log)[:, None] * steps, axis=1)
    running = running - SEGMENT_DROP * (seg - seg_extended[2]).astype(F32)[None, :]
    last = running[:, tokens - 1 :]
    closing = jnp.exp(last - running) * steps
    entering = jnp.exp(running)
    factor = jnp.exp(last[:, 0])
    shape = (heads // STEP_HEADS, STEP_HEADS, tokens)
    col_log = jnp.transpose((running * LOG2E).reshape(shape), (0, 2, 1))
    row_log = (running - jnp.log(steps)) * LOG2E
    close = split_high_low(jnp.transpose(closing.reshape(shape), (0, 2, 1)))
    enter = split_high_low(
        jnp.transpose(entering.reshape(groups, per_group, tokens), (0, 2, 1))
    )

    width = STEP_HEADS * HEAD_DIM
    per_steps = per_group // STEP_HEADS
    pair_width = 2 * STATE_DIM
    step_cols = lambda i: (0, i)
    group_cols = lambda i: (0, i // per_steps)
    y_local, end_state, read_all = pl.pallas_call(
        partial(local_kernel, per_steps),
        grid=(heads // STEP_HEADS,),
        in_specs=[
            pl.BlockSpec((tokens, width), step_cols),
            pl.BlockSpec((HALO, width), step_cols),
            pl.BlockSpec((4, width), step_cols),
            pl.BlockSpec((1, width), step_cols),
            pl.BlockSpec((tokens, pair_width), group_cols),
            pl.BlockSpec((HALO, pair_width), group_cols),
            pl.BlockSpec((4, pair_width), group_cols),
            pl.BlockSpec((1, pair_width), group_cols),
            pl.BlockSpec((tokens, 8), lambda i: (0, 0)),
            pl.BlockSpec((1, tokens, STEP_HEADS), lambda i: (i, 0, 0)),
            pl.BlockSpec((STEP_HEADS, tokens), lambda i: (i, 0)),
            pl.BlockSpec((1, tokens, 2 * STEP_HEADS), lambda i: (i, 0, 0)),
            pl.BlockSpec((1, width), step_cols),
        ],
        out_specs=[
            pl.BlockSpec((tokens, width), step_cols),
            pl.BlockSpec((width, STATE_DIM), lambda i: (i, 0)),
            pl.BlockSpec((tokens, STATE_DIM), group_cols),
        ],
        out_shape=[
            jax.ShapeDtypeStruct((tokens, inner_width), BF16),
            jax.ShapeDtypeStruct((inner_width, STATE_DIM), BF16),
            jax.ShapeDtypeStruct((tokens, groups * STATE_DIM), BF16),
        ],
        scratch_shapes=[
            pltpu.VMEM((tokens, tokens), F32),
            pltpu.VMEM((tokens, STATE_DIM), BF16),
        ],
        compiler_params=pltpu.CompilerParams(vmem_limit_bytes=32 * 2**20),
        cost_estimate=pl.CostEstimate(
            flops=10**6, bytes_accessed=10**6, transcendentals=0
        ),
        name="local_scan",
    )(
        inner_input,
        halo[:, :inner_width],
        inner_taps.astype(F32),
        inner_bias.astype(F32)[None],
        state_input,
        halo[:, inner_width:],
        state_taps.astype(F32),
        state_bias.astype(F32)[None],
        masks,
        col_log,
        row_log,
        close,
        jnp.repeat(skip_gain, HEAD_DIM)[None],
    )

    half = heads // 2
    half_rows = half * HEAD_DIM

    def half_of(value, which):
        return lax.dynamic_slice_in_dim(value, which * (value.shape[0] // 2), value.shape[0] // 2)

    def per_row(value):
        return jnp.repeat(value, HEAD_DIM)[:, None]

    factor_other = swapped(factor)
    mine, other = half_of(end_state, side), half_of(end_state, 1 - side)
    peer_end = swapped(other).astype(F32)
    mine = mine.astype(F32)
    first_end = jnp.where(side == 0, mine, peer_end)
    second_end = jnp.where(side == 0, peer_end, mine)
    first_factor = per_row(half_of(jnp.where(side == 0, factor, factor_other), side))
    second_factor = per_row(half_of(jnp.where(side == 0, factor_other, factor), side))
    pair_total = second_factor * first_end + second_end
    pair_factor = first_factor * second_factor
    window = pair_total
    for hop in range(max(1, seq_count // 4)):
        arriving = moved(window.astype(BF16), 2).astype(F32)
        window = pair_total + pair_factor * arriving
    up[-1], down[-1], arriving = lax.optimization_barrier((up[-1], down[-1], arriving))
    if rows_count > 2:
        up.append(moved(up[-1], 2))
        down.append(moved(down[-1], -2))
    after_first = (first_factor * arriving + first_end).astype(BF16)
    arriving = arriving.astype(BF16)
    own_part = jnp.where(side == 0, arriving, after_first)
    peer_part = swapped(jnp.where(side == 0, after_first, arriving))
    state_low = jnp.where(side == 0, own_part, peer_part)
    state_high = jnp.where(side == 0, peer_part, own_part)
    state_in = jnp.concatenate([state_low, state_high], axis=0)

    gains = norm_gain.astype(F32)[None]
    own, peer = [], []
    for group in range(groups):
        normed = pl.pallas_call(
            norm_kernel,
            grid=(tokens // TILE,),
            in_specs=[
                pl.BlockSpec((TILE, group_width), lambda i, g=group: (i, g)),
                pl.BlockSpec((TILE, group_width), lambda i, g=group: (i, g)),
                pl.BlockSpec((group_width, STATE_DIM), lambda i, g=group: (g, 0)),
                pl.BlockSpec((TILE, STATE_DIM), lambda i, g=group: (i, g)),
                pl.BlockSpec((1, TILE, 2 * per_group), lambda i, g=group: (g, i, 0)),
                pl.BlockSpec((1, group_width), lambda i, g=group: (0, g)),
            ],
            out_specs=pl.BlockSpec((TILE, group_width), lambda i: (i, 0)),
            out_shape=jax.ShapeDtypeStruct((tokens, group_width), BF16),
            scratch_shapes=[pltpu.VMEM((TILE, group_width), F32)],
            compiler_params=pltpu.CompilerParams(vmem_limit_bytes=32 * 2**20),
            cost_estimate=pl.CostEstimate(
                flops=10**6, bytes_accessed=10**6, transcendentals=0
            ),
            name="gated_norm",
        )(y_local, gate_input, state_in, read_all, enter, gains)
        own.append(normed)
        peer.append(swapped(normed))
    acts = own + peer
    zero = (own[-1][:16, :128] + peer[0][:16, :128]) * jnp.zeros((), BF16)
    up[-1] = lax.dynamic_update_slice(up[-1], up[-1][:16, :128] + zero, (0, 0))
    down[-1] = lax.dynamic_update_slice(down[-1], down[-1][:16, :128] + zero, (0, 0))
    for _ in range(rows_count - 3):
        up.append(moved(up[-1], 2))
        down.append(moved(down[-1], -2))

    per_head = rows_count // head_count
    reduced = []
    for distance in range(rows_count):
        if distance == 0:
            one, two, first = out_weight, out_weight, jnp.ones((1,), jnp.int32)
        else:
            one, two = up[distance], down[rows_count - distance]
            first = (row_at >= distance).astype(jnp.int32)[None]
        value = project(acts, one, two, first)
        bit = 1
        while bit < head_count:
            pairs = []
            for s in range(seq_count):
                owner = (s // 2 - distance) % rows_count // per_head
                for h in range(head_count):
                    if h % bit == owner % bit and (h ^ owner) & bit:
                        pairs.append((s * head_count + h, s * head_count + (h ^ bit)))
            got = lax.ppermute(value, ("seq", "head"), pairs)
            value = (value.astype(F32) + got.astype(F32)).astype(BF16)
            bit *= 2
        reduced.append(value)
    finals = []
    for shard in range(per_head):
        wanted = (row_at - head_at * per_head - shard) % rows_count
        chosen = reduced[0]
        for distance in range(1, rows_count):
            chosen = jnp.where(wanted == distance, reduced[distance], chosen)
        finals.append(chosen)
    final = jnp.stack(finals)
    mine_out = final[:, :tokens]
    peer_out = swapped(final[:, tokens:])
    even = jnp.where(side == 0, mine_out, peer_out)
    odd = jnp.where(side == 0, peer_out, mine_out)
    both = jnp.stack([even, odd], axis=1)
    return jnp.transpose(both, (2, 0, 1, 3)).reshape(tokens, -1)


def solution(mesh):
    in_specs = (
        P("seq", "head"),
        P("seq", "head"),
        P("seq", "head"),
        P(None, "head"),
        P("head"),
        P(None, "head"),
        P("head"),
        P("head", "seq"),
        P("head"),
        P("head"),
        P("head"),
        P("head"),
        P("head", "seq"),
        P(),
    )
    out_specs = P("seq", "head")
    return jax.shard_map(
        per_device, mesh=mesh, in_specs=in_specs, out_specs=out_specs, check_vma=False
    )
```
